512 devices in a mesh: gx: 8 (over x, core), gy: 4 (over y), gz: 16 (over z).
Axes of the slice: x: 4, y: 4, z: 16, core: 2. Of those that a mesh axis runs over, the one named last changes fastest.
Arguments:
- flow_state: float32 [8, 4, 16, 5, 4, 128, 128], P('gx', 'gy', 'gz'), may hold values from -2 to 8, as said below
- face_links: int32 [8, 4, 16, 4], P('gx', 'gy', 'gz'), may hold values from 0 to 15, as said below
- donor_plane: int32 [8, 4, 16, 64], P('gx', 'gy', 'gz'), may hold values from 0 to 2
- donor_line: int32 [8, 4, 16, 64], P('gx', 'gy', 'gz'), may hold values from 0 to 126
- donor_weights: float32 [8, 4, 16, 64, 3], P('gx', 'gy', 'gz'), may hold values from 0 to 1
- receptor_owner: int32 [8, 4, 16, 64, 1], P('gx', 'gy', 'gz'), may hold values from 0 to 63; in each aligned block of 64 rows (0 to 63, 64 to 127, ..., all dimensions but the last counted through in order) at most 2 rows name the same one
Outputs:
- new_state: float32 [8, 4, 16, 5, 4, 128, 128], P('gx', 'gy', 'gz')
- fringe: float32 [8, 4, 16, 128, 640], P('gx', 'gy', 'gz')
The draws below stay inside these ranges and needn't reach their ends.
Inputs may be any that keep to these rules, and one draw needn't show every extreme that they name: `flow_state`: the state of every cell has density in [0.5, 2], velocity components in [-1, 1] and pressure in [0.5, 2]. face_links holds indices along the third block index within the same column of blocks and flags 0 or 1; in each column the k-high links form one closed loop through all 16 blocks, and a block's k-high neighbour has that block as its k-low neighbour with the same flag. `receptor_owner`: among the donor lines of one block no owner is named more than 2 times, a bound that some block reaches.
All inputs are finite; a program needn't handle non-finite values.
Results may differ from the reference program's by a relative error of at most 0.000071.
Values sent between devices are 32-bit elements; how exact they have to be, the bound alone decides.
A program may use at most 128 MiB of HBM per device.

```python
import math
import jax
import jax.numpy as jnp
import numpy as np
from jax import lax

VARS = 5
PL = 4
NJ = 128
NK = 128
DROWS = 64
BX = 8
BY = 4
BZ = 16
GROUP = 64
CAP = 2
SLOTS = 128


GAMMA = 1.4


def draw_flow_state(key, part):
    grid_shape = (BX, BY, BZ, PL, NJ, NK)
    first_key = jax.random.fold_in(key, 11)
    second_key = jax.random.fold_in(key, 12)
    third_key = jax.random.fold_in(key, 13)
    spread = math.log(2.0)
    density = jnp.exp(jax.random.uniform(first_key, grid_shape, jnp.float32, -spread, spread))
    velocity = jnp.clip(0.4 * jax.random.normal(second_key, (3,) + grid_shape, jnp.float32), -1.0, 1.0)
    pressure = jnp.exp(jax.random.uniform(third_key, grid_shape, jnp.float32, -spread, spread))
    momentum = density[None] * velocity
    energy = pressure / (GAMMA - 1.0) + 0.5 * density * jnp.sum(velocity * velocity, axis=0)
    stacked = jnp.concatenate([density[None], momentum, energy[None]], axis=0)
    return jnp.moveaxis(stacked, 0, 3).astype(jnp.float32)


def draw_face_links(key, part):
    columns = BX * BY

    def one_column(column_index):
        column_key = jax.random.fold_in(jax.random.fold_in(key, 21), column_index)
        loop_order = jax.random.permutation(jax.random.fold_in(column_key, 1), BZ).astype(jnp.int32)
        flip_flags = jax.random.randint(jax.random.fold_in(column_key, 2), (BZ,), 0, 2).astype(jnp.int32)
        after = jnp.roll(loop_order, -1)
        before = jnp.roll(loop_order, 1)
        flags_before = jnp.roll(flip_flags, 1)
        link_rows = jnp.stack([before, flags_before, after, flip_flags], axis=1)
        return jnp.zeros((BZ, 4), jnp.int32).at[loop_order].set(link_rows)
    link_table = jax.vmap(one_column)(jnp.arange(columns, dtype=jnp.int32))
    return link_table.reshape(BX, BY, BZ, 4).astype(jnp.int32)


def place_ends(array, stream_key, smallest, top_value):
    place = [jax.random.randint(jax.random.fold_in(stream_key, axis), (), 0, length) for axis, length in enumerate(array.shape)]
    widest = array.shape.index(max(array.shape))
    beside = place[:widest] + [(place[widest] + 1) % array.shape[widest]] + place[widest + 1:]
    return array.at[tuple(place)].set(smallest).at[tuple(beside)].set(top_value)


def block_levels(key, dims, cuts, low, largest):
    def one(axis_at, blocks):
        steps = jax.random.uniform(jax.random.fold_in(jax.random.fold_in(key, 6), axis_at), (blocks,), jnp.float32, low / len(cuts), largest / len(cuts))
        return jnp.repeat(jnp.exp(steps), dims[axis_at] // blocks).reshape((-1,) + (1,) * (len(dims) - axis_at - 1))

    loudness = one(*cuts[0])
    for cut in cuts[1:]:
        loudness = loudness * one(*cut)
    return loudness


def deal_out(stream_key, own, number, rows, count, top, reach, slope):
    ranking = jax.random.permutation(stream_key, count)
    heavy_load, usual = load_shares(count, rows * top, reach, slope, True), load_shares(count, rows * top, reach, slope, False)
    places = jnp.arange(count)

    def named(tallies, turn):
        used = int((tallies > 0).sum())
        fixed = max(1, used // 4)
        passed = fixed + (places - fixed + turn * (used - fixed)) % max(1, count - fixed)
        return jnp.zeros((count,), jnp.int32).at[ranking[jnp.where(places < fixed, places, passed)]].set(jnp.asarray(tallies, jnp.int32))

    tallies = jnp.where(number % 4 == 0, named(heavy_load, number // 4), named(usual, number - number // 4 - 1))
    mixed = jax.random.permutation(jax.random.fold_in(own, 3), count)
    giver, receiver = mixed[0:count // 2 * 2:2], mixed[1:count // 2 * 2:2]
    margin = jnp.minimum(tallies[giver] - 1, reach - tallies[receiver]) // 2
    margin = jnp.where((giver == ranking[0]) | (receiver == ranking[0]) | (tallies[receiver] == 0), 0, jnp.maximum(margin, 0))
    passed = jax.random.randint(jax.random.fold_in(own, 4), (count // 2,), 0, 1 << 20) % (margin + 1)
    tallies = tallies.at[giver].add(-passed).at[receiver].add(passed)
    labels = jnp.searchsorted(jnp.cumsum(tallies), jnp.arange(rows * top), side="right").astype(jnp.int32)
    grid = labels.reshape(top, rows).T
    grid = grid[jax.random.permutation(jax.random.fold_in(own, 1), rows)]
    turn = jax.random.randint(jax.random.fold_in(own, 2), (rows, 1), 0, top)
    return jnp.take_along_axis(grid, (jnp.arange(top)[None, :] + turn) % top, axis=1)


def load_shares(number_of, total, most, lean, full):
    weights = [(1 << 20) // math.isqrt(standing ** lean) + 1 for standing in range(1, number_of + 1)]
    largest = most if full else min(most, max(-(-total // number_of), total * weights[0] // sum(weights)))
    least = 1 if total - largest >= number_of - 1 else 0
    holding, spare = [largest] + [least] * (number_of - 1), total - largest - least * (number_of - 1)
    while spare > 0:
        candidates = [i for i in range(1, number_of) if holding[i] < largest] or [i for i in range(1, number_of) if holding[i] < most]
        pool, budget = sum([weights[i] for i in candidates]), spare
        for i in candidates:
            addition = min(most - holding[i], max(1, budget * weights[i] // pool), spare)
            holding[i] = holding[i] + addition
            spare = spare - addition
    return np.array(holding)


def setup_inputs(seed: int = 0) -> dict:
    key_list = jax.random.split(jax.random.key(seed), 7)
    flow_state = draw_flow_state(jax.random.fold_in(key_list[6], 71), 0)
    face_links = draw_face_links(jax.random.fold_in(key_list[6], 71), 0)
    donor_plane = place_ends(jax.random.randint(key_list[2], (BX, BY, BZ, DROWS), 0, PL - 1), jax.random.fold_in(key_list[2], 1), 0, (PL - 1) - 1).astype(jnp.int32)
    donor_line = place_ends(jax.random.randint(key_list[3], (BX, BY, BZ, DROWS), 0, NJ - 1), jax.random.fold_in(key_list[3], 1), 0, (NJ - 1) - 1).astype(jnp.int32)
    donor_weights = jnp.clip(1.0 * jax.random.uniform(key_list[4], (BX, BY, BZ, DROWS, 3), jnp.float32) ** block_levels(key_list[4], (BX, BY, BZ, DROWS, 3), ((0, 8), (1, 4), (2, 16)), -0.2, 0.2), 0.0, 1.0)
    receptor_owner_keys = jax.random.split(jax.random.fold_in(key_list[5], 1), BX * BY * BZ * DROWS // DROWS)
    receptor_owner_turns = jax.random.permutation(jax.random.fold_in(key_list[5], 3), BX * BY * BZ * DROWS // DROWS)
    receptor_owner = jax.vmap(lambda own, number: deal_out(jax.random.fold_in(key_list[5], 2), own, number, DROWS, GROUP, 1, CAP, 2))(receptor_owner_keys, receptor_owner_turns).reshape((BX, BY, BZ, DROWS, 1))
    return {"flow_state": flow_state, "face_links": face_links, "donor_plane": donor_plane, "donor_line": donor_line, "donor_weights": donor_weights, "receptor_owner": receptor_owner}


GAMMA = 1.4
DT_DX = 0.08

def cell_fluxes(values, direction):
    density = values[0]
    momentum = values[1:4]
    energy = values[4]
    velocity = momentum / density
    pressure = (GAMMA - 1.0) * (energy - 0.5 * lax.optimization_barrier(jnp.sum(momentum * velocity, axis=0)))
    sound_speed = jnp.sqrt(GAMMA * pressure / density)
    normal_speed = velocity[direction]
    pieces = [momentum[direction]]
    for component in range(3):
        term = momentum[component] * normal_speed
        if component == direction:
            term = term + pressure
        pieces.append(term)
    pieces.append((energy + pressure) * normal_speed)
    return (jnp.stack(pieces), jnp.abs(normal_speed) + sound_speed)

def edge_pad(values, axis_index):
    count = values.shape[axis_index]
    first = lax.slice_in_dim(values, 0, 1, axis=axis_index)
    last = lax.slice_in_dim(values, count - 1, count, axis=axis_index)
    return jnp.concatenate([first, values, last], axis=axis_index)

def face_flux(padded, direction):
    axis_index = direction + 1
    count = padded.shape[axis_index]
    cell_flux, speed = cell_fluxes(padded, direction)
    left_flux = lax.slice_in_dim(cell_flux, 0, count - 1, axis=axis_index)
    right_flux = lax.slice_in_dim(cell_flux, 1, count, axis=axis_index)
    left_speed = lax.slice_in_dim(speed, 0, count - 1, axis=direction)
    right_speed = lax.slice_in_dim(speed, 1, count, axis=direction)
    left_state = lax.slice_in_dim(padded, 0, count - 1, axis=axis_index)
    right_state = lax.slice_in_dim(padded, 1, count, axis=axis_index)
    return 0.5 * (left_flux + right_flux) - 0.5 * jnp.maximum(left_speed, right_speed) * (right_state - left_state)

def difference(faces_flux, axis_index):
    count = faces_flux.shape[axis_index]
    return lax.slice_in_dim(faces_flux, 1, count, axis=axis_index) - lax.slice_in_dim(faces_flux, 0, count - 1, axis=axis_index)

def advance_section(local_block, low_ghost, high_ghost):
    extended = jnp.concatenate([low_ghost[..., None], local_block, high_ghost[..., None]], axis=3)
    change = difference(face_flux(edge_pad(local_block, 1), 0), 1)
    change = change + difference(face_flux(edge_pad(local_block, 2), 1), 2)
    change = change + difference(face_flux(extended, 2), 3)
    return (local_block - DT_DX * change, extended)

def interpolate(extended, donor_plane, donor_line, donor_weights):
    count = extended.shape[3] - 2
    plane_frac = donor_weights[:, 0][:, None, None]
    line_frac = donor_weights[:, 1][:, None, None]
    cell_frac = donor_weights[:, 2][:, None, None]
    summed = jnp.zeros((donor_plane.shape[0], extended.shape[0], count), jnp.float32)
    for plane_step in range(2):
        plane_weight = plane_frac if plane_step == 1 else 1.0 - plane_frac
        for line_step in range(2):
            line_weight = line_frac if line_step == 1 else 1.0 - line_frac
            picked = extended[:, donor_plane + plane_step, donor_line + line_step, :]
            picked = jnp.transpose(picked, (1, 0, 2))
            inner = (1.0 - cell_frac) * picked[:, :, 1:count + 1] + cell_frac * picked[:, :, 2:count + 2]
            summed = summed + plane_weight * line_weight * inner
    return summed

def reference(flow_state, face_links, donor_plane, donor_line, donor_weights, receptor_owner):
    last_layer = flow_state[..., -1]
    first_layer = flow_state[..., 0]

    def neighbour(layer, column, flag):
        index_table = face_links[..., column][:, :, :, None, None, None]
        index_table = jnp.broadcast_to(index_table, layer.shape).astype(jnp.int32)
        picked = jnp.take_along_axis(layer, index_table, axis=2)
        flipped = face_links[..., flag][:, :, :, None, None, None] == 1
        return jnp.where(flipped, jnp.flip(picked, -1), picked)
    low_ghost = neighbour(last_layer, 0, 1)
    high_ghost = neighbour(first_layer, 2, 3)
    blocks = BX * BY * BZ

    def one_block(items):
        local_block, low, high, plane, line, weights = items
        updated, extended = advance_section(local_block, low, high)
        return (updated, interpolate(extended, plane, line, weights))
    updated, row_values = lax.map(one_block, (flow_state.reshape(blocks, VARS, PL, NJ, NK), low_ghost.reshape(blocks, VARS, PL, NJ), high_ghost.reshape(blocks, VARS, PL, NJ), donor_plane.reshape(blocks, DROWS), donor_line.reshape(blocks, DROWS), donor_weights.reshape(blocks, DROWS, 3)))
    new_state = updated.reshape(flow_state.shape)
    row_values = row_values.reshape(BX, GROUP, DROWS, VARS * NK)
    owners = receptor_owner.reshape(BX, GROUP, DROWS).astype(jnp.int32)
    onehot = (owners[..., None] == jnp.arange(GROUP, dtype=jnp.int32)).astype(jnp.int32)
    earlier = (jnp.cumsum(onehot, axis=2) - onehot).astype(jnp.int32)
    rank_order = lax.optimization_barrier(jnp.sum(onehot * earlier, axis=3)).astype(jnp.int32)
    source = jnp.arange(GROUP, dtype=jnp.int32)[None, :, None]
    slot_index = (source * CAP + rank_order).astype(jnp.int32)
    column_index = jnp.broadcast_to(jnp.arange(BX, dtype=jnp.int32)[:, None, None], owners.shape)
    fringe = jnp.zeros((BX, GROUP, SLOTS, VARS * NK), jnp.float32)
    fringe = fringe.at[column_index, owners, slot_index].set(row_values)
    return (new_state, fringe.reshape(BX, BY, BZ, SLOTS, VARS * NK))
```

```python
import jax
import jax.numpy as jnp
from jax import lax
from jax.experimental import pallas as pl
from jax.experimental.pallas import tpu as pltpu
from jax.sharding import PartitionSpec as P

MESH = pl.DeviceIdType.MESH
EXACT = lax.Precision.HIGHEST
NY, NZ, QUAD = 4, 16, 4
GROUP, CAP = 64, 2
VARS, PL, NJ, NK = 5, 4, 128, 128
LINES = 64
PAD = 8
WIDE = VARS * NK
FACE_ROWS = 24
F32 = jnp.float32


def iota(shape, dim):
    return lax.broadcasted_iota(jnp.int32, shape, dim)


def prims(u):
    r = 1.0 / u[0]
    vel = [u[1] * r, u[2] * r, u[3] * r]
    kinetic = u[1] * vel[0] + u[2] * vel[1] + u[3] * vel[2]
    p = 0.4 * (u[4] - 0.5 * kinetic)
    return vel, p, jnp.sqrt(1.4 * p * r)


def flux(u, prim, d):
    vel, p, cs = prim
    n = vel[d]
    f = [u[1 + d]]
    for c in range(3):
        t = u[1 + c] * n
        f.append(t + p if c == d else t)
    f.append((u[4] + p) * n)
    return f, jnp.abs(n) + cs


def face(left, right):
    (ul, fl, sl), (ur, fr, sr) = left, right
    a = jnp.maximum(sl, sr)
    return [0.5 * (fl[v] + fr[v]) - 0.5 * a * (ur[v] - ul[v]) for v in range(VARS)]


def side(u, d):
    f, s = flux(u, prims(u), d)
    return u, f, s


def slot_matrix(dplane, dline, weights, owner):
    own_col = owner[...].astype(F32)
    earlier = iota((LINES, LINES), 0)
    later = iota((LINES, LINES), 1)
    diag = earlier == later

    def as_row(col):
        return jnp.sum(jnp.where(diag, col, 0.0), axis=0, keepdims=True)

    own_row = as_row(own_col)
    rank_row = jnp.sum(
        jnp.where((own_col == own_row) & (earlier < later), 1.0, 0.0), axis=0, keepdims=True
    )
    slot_row = CAP * own_row + rank_row
    chosen = iota((GROUP * CAP, LINES), 0).astype(F32) == slot_row

    def pick(row):
        return jnp.sum(jnp.where(chosen, row, 0.0), axis=1, keepdims=True)

    w = weights[...]
    q = pick(dplane[...].astype(F32))
    j = pick(dline[...].astype(F32))
    a1 = pick(as_row(w[:, 0:1]))
    a2 = pick(as_row(w[:, 1:2]))
    a3 = pick(as_row(w[:, 2:3]))
    used = pick(jnp.ones((1, LINES), F32))
    lane = iota((GROUP * CAP, NJ), 1).astype(F32)
    along_j = jnp.where(lane == j, 1.0 - a2, 0.0) + jnp.where(lane == j + 1.0, a2, 0.0)
    along_j = along_j * used
    parts = []
    for plane in range(PL):
        weight = jnp.where(q == plane, 1.0 - a1, 0.0) + jnp.where(q + 1.0 == plane, a1, 0.0)
        parts.append(weight * along_j)
    return parts, a3


def exchange_kernel(
    flow, links_in, dplane_in, dline_in, weights_in, owner_in,
    state, arrived,
    cells, links, dplane, dline, weights, owner,
    faces, chosen, got, ghost_lo, ghost_hi, sending, slots, rows, fracs,
    in_sem, s1_send, s1_recv, s2_send, s2_recv, m_send, m_recv,
):
    y = lax.axis_index("gy")
    z = lax.axis_index("gz")
    me = y * NZ + z
    a, b = z % QUAD, z // QUAD

    loads = [
        pltpu.make_async_copy(flow, cells.at[:, :, pl.ds(PAD, NJ), :], in_sem.at[0]),
        pltpu.make_async_copy(links_in, links, in_sem.at[1]),
        pltpu.make_async_copy(dplane_in, dplane, in_sem.at[2]),
        pltpu.make_async_copy(dline_in, dline, in_sem.at[3]),
        pltpu.make_async_copy(weights_in, weights, in_sem.at[4]),
        pltpu.make_async_copy(owner_in, owner, in_sem.at[5]),
    ]
    for load in loads:
        load.start()

    def peer(t):
        py = (y + t // NZ) % NY
        pz = (z + t) % NZ
        return py, pz

    barrier = pltpu.get_barrier_semaphore()

    def greet(t, carry):
        py, pz = peer(t)
        pl.semaphore_signal(barrier, inc=1, device_id={"gy": py, "gz": pz}, device_id_type=MESH)
        return carry

    lax.fori_loop(1, GROUP, greet, 0)

    for load in loads:
        load.wait()

    first_last = iota((8, NK), 0)
    lane8 = iota((8, NK), 1)
    ends = jnp.where(
        ((first_last == 0) & (lane8 == 0)) | ((first_last == 1) & (lane8 == NK - 1)), 1.0, 0.0
    )
    for v in range(VARS):
        for p in range(PL):
            layer = lax.dot_general(
                ends, cells[v, p, pl.ds(PAD, NJ), :], (((1,), (1,)), ((), ())),
                precision=EXACT, preferred_element_type=F32,
            )
            faces[0, 0, pl.ds(v * PL + p, 1), :] = layer[0:1]
            faces[0, 1, pl.ds(v * PL + p, 1), :] = layer[1:2]
    for r in range(2):
        goal = jnp.full((4, NJ), links[0, 2 * r], jnp.int32).astype(F32)
        faces[0, r, pl.ds(VARS * PL, 4), :] = goal

    pl.semaphore_wait(barrier, GROUP - 1)

    stage1 = []
    for s in range(1, QUAD):
        stage1.append(pltpu.make_async_remote_copy(
            src_ref=faces.at[0], dst_ref=faces.at[s],
            send_sem=s1_send.at[s], recv_sem=s1_recv.at[s],
            device_id={"gy": y, "gz": b * QUAD + (a + s) % QUAD}, device_id_type=MESH,
        ))
        stage1[-1].start()

    parts, a3 = slot_matrix(dplane, dline, weights, owner)
    for plane in range(PL):
        slots[:, pl.ds(plane * NJ, NJ)] = parts[plane]
    fracs[...] = jnp.broadcast_to(a3, (GROUP * CAP, NK))
    for v in range(VARS):
        lines = cells[v, :, pl.ds(PAD, NJ), :].reshape(PL * NJ, NK)
        rows[:, pl.ds(v * NK, NK)] = jnp.dot(
            slots[...], lines, precision=EXACT, preferred_element_type=F32
        )
        for p in range(PL):
            cells[v, p, pl.ds(PAD - 1, 1), :] = cells[v, p, pl.ds(PAD, 1), :]
            cells[v, p, pl.ds(PAD + NJ, 1), :] = cells[v, p, pl.ds(PAD + NJ - 1, 1), :]

    for copy in stage1:
        copy.wait()

    stage2 = []
    for s in list(range(1, QUAD)) + [0]:
        goal = (((b + s) % QUAD) * QUAD + a).astype(F32)
        for r in range(2):
            total = jnp.zeros((FACE_ROWS, NJ), F32)
            for source in range(QUAD):
                tag = faces[source, r, pl.ds(VARS * PL, 1), :]
                total = total + jnp.where(tag == goal, faces[source, r], 0.0)
            if s:
                chosen[s, r] = total
            else:
                got[0, r] = total
        if s:
            stage2.append(pltpu.make_async_remote_copy(
                src_ref=chosen.at[s], dst_ref=got.at[s],
                send_sem=s2_send.at[s], recv_sem=s2_recv.at[s],
                device_id={"gy": y, "gz": ((b + s) % QUAD) * QUAD + a}, device_id_type=MESH,
            ))
            stage2[-1].start()
    for copy in stage2:
        copy.wait()

    down = iota((NJ, NJ), 0)
    across = iota((NJ, NJ), 1)
    for r, ghost, column in ((0, ghost_hi, 3), (1, ghost_lo, 1)):
        layer = (got[0, r] + got[1, r]) + (got[2, r] + got[3, r])
        flipped = jnp.full((NJ, NJ), links[0, column], jnp.int32) == 1
        turn = jnp.where(across == jnp.where(flipped, NJ - 1 - down, down), 1.0, 0.0)
        ghost[...] = lax.dot_general(
            turn, layer, (((1,), (1,)), ((), ())), precision=EXACT, preferred_element_type=F32
        )

    lane_face = iota((GROUP * CAP, FACE_ROWS), 1)
    beyond = jnp.zeros((GROUP * CAP, FACE_ROWS), F32)
    for plane in range(PL):
        term = jnp.dot(
            slots[:, pl.ds(plane * NJ, NJ)], ghost_hi[...],
            precision=EXACT, preferred_element_type=F32,
        )
        beyond = beyond + jnp.where(lane_face % PL == plane, term, 0.0)
    lane = iota((GROUP * CAP, NK), 1)
    frac = fracs[...]
    for v in range(VARS):
        here = rows[:, pl.ds(v * NK, NK)]
        tail = jnp.sum(jnp.where(lane_face // PL == v, beyond, 0.0), axis=1, keepdims=True)
        following = jnp.where(lane == NK - 1, tail, pltpu.roll(here, NK - 1, 1))
        value = (1.0 - frac) * here + frac * following
        sending[:, :, pl.ds(v * NK, NK)] = value.reshape(GROUP, CAP, NK)

    def send(t, carry):
        py, pz = peer(t)
        pltpu.make_async_remote_copy(
            src_ref=sending.at[py * NZ + pz], dst_ref=arrived.at[me],
            send_sem=m_send, recv_sem=m_recv,
            device_id={"gy": py, "gz": pz}, device_id_type=MESH,
        ).start()
        return carry

    lax.fori_loop(1, GROUP, send, 0)
    arrived[me] = sending[me]

    lane_k = iota((8, NK), 1)

    def advance(jb, carry):
        at = pl.multiple_of(jb * 8, 8)

        def load(p, shift):
            return [cells[v, p, pl.ds(at + PAD + shift, 8), :] for v in range(VARS)]

        lo = ghost_lo[pl.ds(at, 8), :]
        hi = ghost_hi[pl.ds(at, 8), :]
        centre = [load(p, 0) for p in range(PL)]
        prim = [prims(u) for u in centre]
        across = [(centre[p],) + flux(centre[p], prim[p], 0) for p in range(PL)]
        edges = [across[0][1]]
        for p in range(PL - 1):
            edges.append(face(across[p], across[p + 1]))
        edges.append(across[PL - 1][1])
        for p in range(PL):
            u = centre[p]
            change = [edges[p + 1][v] - edges[p][v] for v in range(VARS)]
            mid = (u,) + flux(u, prim[p], 1)
            after = face(mid, side(load(p, 1), 1))
            before = face(side(load(p, -1), 1), mid)
            change = [change[v] + (after[v] - before[v]) for v in range(VARS)]
            mid = (u,) + flux(u, prim[p], 2)
            right = [
                jnp.where(lane_k == NK - 1, hi[:, v * PL + p : v * PL + p + 1], pltpu.roll(u[v], NK - 1, 1))
                for v in range(VARS)
            ]
            left = [
                jnp.where(lane_k == 0, lo[:, v * PL + p : v * PL + p + 1], pltpu.roll(u[v], 1, 1))
                for v in range(VARS)
            ]
            after = face(mid, side(right, 2))
            before = face(side(left, 2), mid)
            change = [change[v] + (after[v] - before[v]) for v in range(VARS)]
            for v in range(VARS):
                state[v, p, pl.ds(at, 8), :] = u[v] - 0.08 * change[v]
        return carry

    lax.fori_loop(0, NJ // 8, advance, 0)

    others = pl.ds(0, GROUP - 1)
    pltpu.make_async_copy(arrived.at[others], arrived.at[others], m_recv).wait()
    pltpu.make_async_copy(sending.at[others], sending.at[others], m_send).wait()


def finish_kernel(state_in, arrived, state_out, fringe, sem):
    copy = pltpu.make_async_copy(state_in, state_out, sem)
    copy.start()
    for g in range(GROUP):
        fringe[pl.ds(CAP * g, CAP), :] = arrived[g]
    copy.wait()


def local(flow_state, face_links, donor_plane, donor_line, donor_weights, receptor_owner):
    anywhere = pl.BlockSpec(memory_space=pl.ANY)
    vmem = pl.BlockSpec(memory_space=pltpu.VMEM)
    state, arrived = pl.pallas_call(
        exchange_kernel,
        out_shape=(
            jax.ShapeDtypeStruct((VARS, PL, NJ, NK), F32),
            jax.ShapeDtypeStruct((GROUP, CAP, WIDE), F32),
        ),
        in_specs=[anywhere] * 6,
        out_specs=(vmem, vmem),
        scratch_shapes=[
            pltpu.VMEM((VARS, PL, NJ + 2 * PAD, NK), F32),
            pltpu.SMEM((1, 4), jnp.int32),
            pltpu.VMEM((1, LINES), jnp.int32),
            pltpu.VMEM((1, LINES), jnp.int32),
            pltpu.VMEM((LINES, 3), F32),
            pltpu.VMEM((LINES, 1), jnp.int32),
            pltpu.VMEM((QUAD, 2, FACE_ROWS, NJ), F32),
            pltpu.VMEM((QUAD, 2, FACE_ROWS, NJ), F32),
            pltpu.VMEM((QUAD, 2, FACE_ROWS, NJ), F32),
            pltpu.VMEM((NJ, FACE_ROWS), F32),
            pltpu.VMEM((NJ, FACE_ROWS), F32),
            pltpu.VMEM((GROUP, CAP, WIDE), F32),
            pltpu.VMEM((GROUP * CAP, PL * NJ), F32),
            pltpu.VMEM((GROUP * CAP, WIDE), F32),
            pltpu.VMEM((GROUP * CAP, NK), F32),
            pltpu.SemaphoreType.DMA((6,)),
            pltpu.SemaphoreType.DMA((QUAD,)),
            pltpu.SemaphoreType.DMA((QUAD,)),
            pltpu.SemaphoreType.DMA((QUAD,)),
            pltpu.SemaphoreType.DMA((QUAD,)),
            pltpu.SemaphoreType.DMA,
            pltpu.SemaphoreType.DMA,
        ],
        compiler_params=pltpu.CompilerParams(
            collective_id=0, has_side_effects=True, vmem_limit_bytes=24 * 1024 * 1024
        ),
    )(
        flow_state.reshape(VARS, PL, NJ, NK),
        face_links.reshape(1, 4),
        donor_plane.reshape(1, LINES),
        donor_line.reshape(1, LINES),
        donor_weights.reshape(LINES, 3),
        receptor_owner.reshape(LINES, 1),
    )
    new_state, fringe = pl.pallas_call(
        finish_kernel,
        out_shape=(
            jax.ShapeDtypeStruct((VARS, PL, NJ, NK), F32),
            jax.ShapeDtypeStruct((GROUP * CAP, WIDE), F32),
        ),
        in_specs=[anywhere, vmem],
        out_specs=(anywhere, vmem),
        scratch_shapes=[pltpu.SemaphoreType.DMA],
        compiler_params=pltpu.CompilerParams(vmem_limit_bytes=16 * 1024 * 1024),
    )(state, arrived)
    return (
        new_state.reshape(1, 1, 1, VARS, PL, NJ, NK),
        fringe.reshape(1, 1, 1, GROUP * CAP, WIDE),
    )


def solution(mesh):
    return jax.shard_map(
        local,
        mesh=mesh,
        in_specs=(
            P("gx", "gy", "gz", None, None, None, None),
            P("gx", "gy", "gz", None),
            P("gx", "gy", "gz", None),
            P("gx", "gy", "gz", None),
            P("gx", "gy", "gz", None, None),
            P("gx", "gy", "gz", None, None),
        ),
        out_specs=(P("gx", "gy", "gz", None, None, None, None), P("gx", "gy", "gz", None, None)),
        check_vma=False,
    )
```

```python
import jax
import jax.numpy as jnp
from jax import lax
from jax.experimental import pallas as pl
from jax.experimental.pallas import tpu as pltpu
from jax.sharding import PartitionSpec as P

MESH = pl.DeviceIdType.MESH
EXACT = lax.Precision.HIGHEST
NY, NZ, QUAD = 4, 16, 4
HALF = NZ // 2
GROUP, CAP = 64, 2
EARLY = 16
VARS, PL, NJ, NK = 5, 4, 128, 128
LINES = 64
PAD = 8
WIDE = VARS * NK
FACE_ROWS = 24
F32 = jnp.float32
ROOM = 60 * 1024 * 1024


def iota(shape, dim):
    return lax.broadcasted_iota(jnp.int32, shape, dim)


def prims(u):
    r = 1.0 / u[0]
    vel = [u[1] * r, u[2] * r, u[3] * r]
    kinetic = u[1] * vel[0] + u[2] * vel[1] + u[3] * vel[2]
    p = 0.4 * (u[4] - 0.5 * kinetic)
    return vel, p, jnp.sqrt(1.4 * p * r)


def flux(u, prim, d):
    vel, p, cs = prim
    n = vel[d]
    f = [u[1 + d]]
    for c in range(3):
        t = u[1 + c] * n
        f.append(t + p if c == d else t)
    f.append((u[4] + p) * n)
    return f, jnp.abs(n) + cs


def face(left, right):
    (ul, fl, sl), (ur, fr, sr) = left, right
    a = jnp.maximum(sl, sr)
    return [0.5 * (fl[v] + fr[v]) - 0.5 * a * (ur[v] - ul[v]) for v in range(VARS)]


def side(u, d):
    f, s = flux(u, prims(u), d)
    return u, f, s


def line_fields(dplane, dline, weights, owner):
    own_row = owner[...].astype(F32)
    earlier = iota((LINES, LINES), 0)
    later = iota((LINES, LINES), 1)
    own_col = jnp.sum(jnp.where(earlier == later, own_row, 0.0), axis=1, keepdims=True)
    rank_row = jnp.sum(
        jnp.where((own_col == own_row) & (earlier < later), 1.0, 0.0), axis=0, keepdims=True
    )
    slot_row = CAP * own_row + rank_row
    return [
        slot_row, dplane[...].astype(F32), dline[...].astype(F32), weights[0], weights[1], weights[2]
    ]


def slot_matrix(fields, lane):
    slot_row = fields[0]
    chosen = iota((GROUP * CAP, LINES), 0).astype(F32) == slot_row

    def pick(row):
        return jnp.sum(jnp.where(chosen, row, 0.0), axis=1, keepdims=True)

    q, j, a1, a2, a3 = [pick(row) for row in fields[1:]]
    used = pick(jnp.ones((1, LINES), F32))
    along_j = jnp.where(lane == j, 1.0 - a2, 0.0) + jnp.where(lane == j + 1.0, a2, 0.0)
    along_j = along_j * used
    parts = []
    for plane in range(PL):
        weight = jnp.where(q == plane, 1.0 - a1, 0.0) + jnp.where(q + 1.0 == plane, a1, 0.0)
        parts.append(weight * along_j)
    return parts, a3


def exchange_kernel(
    flow, links_in, dplane_in, dline_in, weights_in, owner_in,
    state_out, fringe_out,
    state, arrived, fringe, cells, links, dplane, dline, weights, owner,
    faces, chosen, got, ghost_lo, ghost_hi, sending, slots, rows, fracs, ends_out, ends_in, notes,
    in_sem, s1_send, s1_recv, s2_send, s2_recv, m_send, m_recv, e_send, e_recv, n_send, n_recv, out_sem,
):
    y = lax.axis_index("gy")
    z = lax.axis_index("gz")
    me = y * NZ + z
    a, b = z % QUAD, z // QUAD

    loads = [
        pltpu.make_async_copy(flow, cells.at[:, :, pl.ds(PAD, NJ), :], in_sem.at[0]),
        pltpu.make_async_copy(links_in, links, in_sem.at[1]),
        pltpu.make_async_copy(dplane_in, dplane, in_sem.at[2]),
        pltpu.make_async_copy(dline_in, dline, in_sem.at[3]),
        pltpu.make_async_copy(weights_in, weights, in_sem.at[4]),
        pltpu.make_async_copy(owner_in, owner, in_sem.at[5]),
    ]
    for load in loads:
        load.start()

    def peer(i):
        d = HALF - (i + 4) // 8
        dz = jnp.where(i % 2 == 0, d, NZ - d)
        dy = jnp.where(d == HALF, i, jnp.where(d == 0, i - 59, (i - 4) // 2))
        return (y + dy) % NY, (z + jnp.where(d == HALF, HALF, dz)) % NZ

    barrier = pltpu.get_barrier_semaphore()

    def greet(i, carry):
        py, pz = peer(i)
        pl.semaphore_signal(barrier, inc=1, device_id={"gy": py, "gz": pz}, device_id_type=MESH)
        return carry

    lax.fori_loop(0, GROUP - 1, greet, 0)

    for load in loads:
        load.wait()

    first_last = iota((8, NK), 0)
    lane8 = iota((8, NK), 1)
    ends = jnp.where(
        ((first_last == 0) & (lane8 == 0)) | ((first_last == 1) & (lane8 == NK - 1)), 1.0, 0.0
    )
    for v in range(VARS):
        for p in range(PL):
            layer = lax.dot_general(
                ends, cells[v, p, pl.ds(PAD, NJ), :], (((1,), (1,)), ((), ())),
                precision=EXACT, preferred_element_type=F32,
            )
            faces[0, 0, pl.ds(v * PL + p, 1), :] = layer[0:1]
            faces[0, 1, pl.ds(v * PL + p, 1), :] = layer[1:2]
    for r in range(2):
        goal = jnp.full((4, NJ), links[0, 2 * r], jnp.int32).astype(F32)
        faces[0, r, pl.ds(VARS * PL, 4), :] = goal

    lane = iota((GROUP * CAP, NK), 1)
    fields = line_fields(dplane, dline, weights, owner)
    lane_f = lane.astype(F32)
    parts, a3 = slot_matrix(fields, lane_f)
    for plane in range(PL):
        slots[:, pl.ds(plane * NJ, NJ)] = parts[plane]
    fracs[...] = jnp.broadcast_to(a3, (GROUP * CAP, NK))
    for v in range(VARS):
        lines = cells[v, :, pl.ds(PAD, NJ), :].reshape(PL * NJ, NK)
        rows[:, pl.ds(v * NK, NK)] = jnp.dot(
            slots[...], lines, precision=EXACT, preferred_element_type=F32
        )
        for p in range(PL):
            cells[v, p, pl.ds(PAD - 1, 1), :] = cells[v, p, pl.ds(PAD, 1), :]
            cells[v, p, pl.ds(PAD + NJ, 1), :] = cells[v, p, pl.ds(PAD + NJ - 1, 1), :]

    target = jnp.full((1, LINES), links[0, 2], jnp.int32).astype(F32)
    held = fields + [target, target]
    for row in range(4):
        notes[z, pl.ds(row, 1), :] = jnp.concatenate(held[2 * row : 2 * row + 2], axis=1)

    frac = fracs[...]
    for v in range(VARS):
        here = rows[:, pl.ds(v * NK, NK)]
        following = jnp.where(lane == NK - 1, 0.0, pltpu.roll(here, NK - 1, 1))
        value = (1.0 - frac) * here + frac * following
        sending[:, :, pl.ds(v * NK, NK)] = value.reshape(GROUP, CAP, NK)

    pl.semaphore_wait(barrier, GROUP - 1)

    def send_notes(d, carry):
        pltpu.make_async_remote_copy(
            src_ref=notes.at[z], dst_ref=notes.at[z], send_sem=n_send, recv_sem=n_recv,
            device_id={"gy": y, "gz": (z + jnp.where(d % 2 == 1, NZ - d // 2, d // 2)) % NZ},
            device_id_type=MESH,
        ).start()
        return carry

    lax.fori_loop(0, NZ - 1, lambda i, c: send_notes(NZ - i, c), 0)
    stage1 = []
    for s in range(1, QUAD):
        stage1.append(pltpu.make_async_remote_copy(
            src_ref=faces.at[0], dst_ref=faces.at[s],
            send_sem=s1_send.at[s], recv_sem=s1_recv.at[s],
            device_id={"gy": y, "gz": b * QUAD + (a + s) % QUAD}, device_id_type=MESH,
        ))
        stage1[-1].start()

    def send(i, carry):
        py, pz = peer(i)
        pltpu.make_async_remote_copy(
            src_ref=sending.at[py * NZ + pz], dst_ref=arrived.at[me],
            send_sem=m_send, recv_sem=m_recv,
            device_id={"gy": py, "gz": pz}, device_id_type=MESH,
        ).start()
        return carry

    lax.fori_loop(0, EARLY, send, 0)
    lane_k = iota((8, NK), 1)

    def load(at, p, shift):
        return [cells[v, p, pl.ds(at + PAD + shift, 8), :] for v in range(VARS)]

    def advance(jb, carry):
        at = pl.multiple_of(jb * 8, 8)
        centre = [load(at, p, 0) for p in range(PL)]
        prim = [prims(u) for u in centre]
        layers = [(centre[p],) + flux(centre[p], prim[p], 0) for p in range(PL)]
        edges = [layers[0][1]]
        for p in range(PL - 1):
            edges.append(face(layers[p], layers[p + 1]))
        edges.append(layers[PL - 1][1])
        for p in range(PL):
            u = centre[p]
            mid = (u,) + flux(u, prim[p], 1)
            after = face(mid, side(load(at, p, 1), 1))
            before = face(side(load(at, p, -1), 1), mid)
            for v in range(VARS):
                change = (edges[p + 1][v] - edges[p][v]) + (after[v] - before[v])
                state[v, p, pl.ds(at, 8), :] = u[v] - 0.08 * change
        return carry

    lax.fori_loop(0, NJ // 8, advance, 0)

    for copy in stage1:
        copy.wait()

    stage2 = []
    for s in list(range(1, QUAD)) + [0]:
        goal = (((b + s) % QUAD) * QUAD + a).astype(F32)
        for r in range(2):
            total = jnp.zeros((FACE_ROWS, NJ), F32)
            for source in range(QUAD):
                tag = faces[source, r, pl.ds(VARS * PL, 1), :]
                total = total + jnp.where(tag == goal, faces[source, r], 0.0)
            if s:
                chosen[s, r] = total
            else:
                got[0, r] = total
        if s:
            stage2.append(pltpu.make_async_remote_copy(
                src_ref=chosen.at[s], dst_ref=got.at[s],
                send_sem=s2_send.at[s], recv_sem=s2_recv.at[s],
                device_id={"gy": y, "gz": ((b + s) % QUAD) * QUAD + a}, device_id_type=MESH,
            ))
            stage2[-1].start()
    in_line = pl.ds(0, NZ - 1)
    pltpu.make_async_copy(notes.at[in_line], notes.at[in_line], n_recv).wait()
    wanted = jnp.zeros((4, 2 * LINES), F32)
    for source in range(NZ):
        note = notes[source]
        wanted = wanted + jnp.where(note[3:4, 0:1] == z.astype(F32), note, 0.0)
    theirs = []
    for row in range(3):
        theirs += [wanted[row : row + 1, 0:LINES], wanted[row : row + 1, LINES:]]
    flipped = jnp.full((GROUP * CAP, NJ), links[0, 1], jnp.int32) == 1
    parts, a3 = slot_matrix(theirs, jnp.where(flipped, NJ - 1.0 - lane_f, lane_f))
    lane_face = iota((GROUP * CAP, FACE_ROWS), 1)
    beyond = jnp.zeros((GROUP * CAP, FACE_ROWS), F32)
    for plane in range(PL):
        term = lax.dot_general(
            parts[plane], faces[0, 0], (((1,), (1,)), ((), ())),
            precision=EXACT, preferred_element_type=F32,
        )
        beyond = beyond + jnp.where(lane_face % PL == plane, term, 0.0)
    last = jnp.where(lane == VARS, jnp.full((GROUP * CAP, NK), links[0, 0], jnp.int32).astype(F32), 0.0)
    for v in range(VARS):
        tail = jnp.sum(jnp.where(lane_face // PL == v, beyond, 0.0), axis=1, keepdims=True)
        last = last + jnp.where(lane == v, a3 * tail, 0.0)
    ends_out[...] = last.reshape(GROUP, CAP, NK)

    def send_ends(i, carry):
        py, pz = peer(i)
        pltpu.make_async_remote_copy(
            src_ref=ends_out.at[py * NZ + pz], dst_ref=ends_in.at[me],
            send_sem=e_send, recv_sem=e_recv,
            device_id={"gy": py, "gz": pz}, device_id_type=MESH,
        ).start()
        return carry

    lax.fori_loop(0, GROUP - 1, send_ends, 0)
    ends_in[me] = ends_out[me]

    lax.fori_loop(EARLY, GROUP - 1, send, 0)
    arrived[me] = sending[me]

    for copy in stage2:
        copy.wait()

    down = iota((NJ, NJ), 0)
    across = iota((NJ, NJ), 1)
    for r, ghost, column in ((0, ghost_hi, 3), (1, ghost_lo, 1)):
        layer = (got[0, r] + got[1, r]) + (got[2, r] + got[3, r])
        flipped = jnp.full((NJ, NJ), links[0, column], jnp.int32) == 1
        turn = jnp.where(across == jnp.where(flipped, NJ - 1 - down, down), 1.0, 0.0)
        ghost[...] = lax.dot_general(
            turn, layer, (((1,), (1,)), ((), ())), precision=EXACT, preferred_element_type=F32
        )

    def advance_k(jb, carry):
        at = pl.multiple_of(jb * 8, 8)
        lo = ghost_lo[pl.ds(at, 8), :]
        hi = ghost_hi[pl.ds(at, 8), :]
        for p in range(PL):
            u = load(at, p, 0)
            mid = side(u, 2)
            right = [
                jnp.where(lane_k == NK - 1, hi[:, v * PL + p : v * PL + p + 1], pltpu.roll(u[v], NK - 1, 1))
                for v in range(VARS)
            ]
            left = [
                jnp.where(lane_k == 0, lo[:, v * PL + p : v * PL + p + 1], pltpu.roll(u[v], 1, 1))
                for v in range(VARS)
            ]
            after = face(mid, side(right, 2))
            before = face(side(left, 2), mid)
            for v in range(VARS):
                old = state[v, p, pl.ds(at, 8), :]
                state[v, p, pl.ds(at, 8), :] = old - 0.08 * (after[v] - before[v])
        return carry

    lax.fori_loop(0, NJ // 8, advance_k, 0)
    put_state = pltpu.make_async_copy(state, state_out, out_sem.at[0])
    put_state.start()

    others = pl.ds(0, GROUP - 1)
    pltpu.make_async_copy(ends_in.at[others], ends_in.at[others], e_recv).wait()
    for g in range(GROUP):
        rows[pl.ds(CAP * g, CAP), pl.ds(0, NK)] = ends_in[g]
    came = rows[:, pl.ds(0, NK)]
    slot = iota((GROUP * CAP, GROUP * CAP), 0)
    place = iota((GROUP * CAP, GROUP * CAP), 1)
    donor_z = jnp.sum(jnp.where(slot == place, came[:, VARS : VARS + 1], 0.0), axis=0, keepdims=True)
    home = place // (CAP * NZ) * (CAP * NZ) + place % CAP
    move = jnp.where(slot.astype(F32) == home.astype(F32) + CAP * donor_z, 1.0, 0.0)
    gained = jnp.dot(move, came, precision=EXACT, preferred_element_type=F32)

    pltpu.make_async_copy(arrived.at[others], arrived.at[others], m_recv).wait()
    for g in range(GROUP):
        fringe[pl.ds(CAP * g, CAP), :] = arrived[g]
    for v in range(VARS):
        here = fringe[:, pl.ds(v * NK, NK)]
        fringe[:, pl.ds(v * NK, NK)] = here + jnp.where(lane == NK - 1, gained[:, v : v + 1], 0.0)
    put_fringe = pltpu.make_async_copy(fringe, fringe_out, out_sem.at[1])
    put_fringe.start()
    pltpu.make_async_copy(sending.at[others], sending.at[others], m_send).wait()
    pltpu.make_async_copy(ends_out.at[others], ends_out.at[others], e_send).wait()
    pltpu.make_async_copy(notes.at[in_line], notes.at[in_line], n_send).wait()
    put_state.wait()
    put_fringe.wait()


def finish_kernel(state_in, fringe_in, state_out, fringe_out, state, fringe, in_sem, out_sem):
    trips = [(fringe_in, fringe, fringe_out)]
    for v in range(VARS):
        trips.append((state_in.at[v], state.at[v], state_out.at[v]))
    inward = [pltpu.make_async_copy(t[0], t[1], in_sem.at[i]) for i, t in enumerate(trips)]
    outward = [pltpu.make_async_copy(t[1], t[2], out_sem.at[i]) for i, t in enumerate(trips)]
    for copy in inward:
        copy.start()
    for first, second in zip(inward, outward):
        first.wait()
        second.start()
    for copy in outward:
        copy.wait()


def local(flow_state, face_links, donor_plane, donor_line, donor_weights, receptor_owner):
    anywhere = pl.BlockSpec(memory_space=pl.ANY)
    state, arrived = pl.pallas_call(
        exchange_kernel,
        out_shape=(
            jax.ShapeDtypeStruct((VARS, PL, NJ, NK), F32),
            jax.ShapeDtypeStruct((GROUP * CAP, WIDE), F32),
        ),
        in_specs=[anywhere] * 6,
        out_specs=(anywhere, anywhere),
        scratch_shapes=[
            pltpu.VMEM((VARS, PL, NJ, NK), F32),
            pltpu.VMEM((GROUP, CAP, WIDE), F32),
            pltpu.VMEM((GROUP * CAP, WIDE), F32),
            pltpu.VMEM((VARS, PL, NJ + 2 * PAD, NK), F32),
            pltpu.SMEM((1, 4), jnp.int32),
            pltpu.VMEM((1, LINES), jnp.int32),
            pltpu.VMEM((1, LINES), jnp.int32),
            pltpu.VMEM((3, 1, LINES), F32),
            pltpu.VMEM((1, LINES), jnp.int32),
            pltpu.VMEM((QUAD, 2, FACE_ROWS, NJ), F32),
            pltpu.VMEM((QUAD, 2, FACE_ROWS, NJ), F32),
            pltpu.VMEM((QUAD, 2, FACE_ROWS, NJ), F32),
            pltpu.VMEM((NJ, FACE_ROWS), F32),
            pltpu.VMEM((NJ, FACE_ROWS), F32),
            pltpu.VMEM((GROUP, CAP, WIDE), F32),
            pltpu.VMEM((GROUP * CAP, PL * NJ), F32),
            pltpu.VMEM((GROUP * CAP, WIDE), F32),
            pltpu.VMEM((GROUP * CAP, NK), F32),
            pltpu.VMEM((GROUP, CAP, NK), F32),
            pltpu.VMEM((GROUP, CAP, NK), F32),
            pltpu.VMEM((NZ, 4, 2 * LINES), F32),
            pltpu.SemaphoreType.DMA((6,)),
            pltpu.SemaphoreType.DMA((QUAD,)),
            pltpu.SemaphoreType.DMA((QUAD,)),
            pltpu.SemaphoreType.DMA((QUAD,)),
            pltpu.SemaphoreType.DMA((QUAD,)),
            pltpu.SemaphoreType.DMA,
            pltpu.SemaphoreType.DMA,
            pltpu.SemaphoreType.DMA,
            pltpu.SemaphoreType.DMA,
            pltpu.SemaphoreType.DMA,
            pltpu.SemaphoreType.DMA,
            pltpu.SemaphoreType.DMA((2,)),
        ],
        compiler_params=pltpu.CompilerParams(
            collective_id=0, has_side_effects=True, vmem_limit_bytes=ROOM
        ),
    )(
        flow_state.reshape(VARS, PL, NJ, NK),
        face_links.reshape(1, 4),
        donor_plane.reshape(1, LINES),
        donor_line.reshape(1, LINES),
        jnp.transpose(donor_weights, (0, 1, 4, 2, 3)).reshape(3, 1, LINES),
        receptor_owner.reshape(1, LINES),
    )
    new_state, fringe = pl.pallas_call(
        finish_kernel,
        out_shape=(
            jax.ShapeDtypeStruct((VARS, PL, NJ, NK), F32),
            jax.ShapeDtypeStruct((GROUP * CAP, WIDE), F32),
        ),
        in_specs=[anywhere, anywhere],
        out_specs=(anywhere, anywhere),
        scratch_shapes=[
            pltpu.VMEM((VARS, PL, NJ, NK), F32),
            pltpu.VMEM((GROUP * CAP, WIDE), F32),
            pltpu.SemaphoreType.DMA((1 + VARS,)),
            pltpu.SemaphoreType.DMA((1 + VARS,)),
        ],
        compiler_params=pltpu.CompilerParams(vmem_limit_bytes=ROOM),
    )(state, arrived)
    return (
        new_state.reshape(1, 1, 1, VARS, PL, NJ, NK),
        fringe.reshape(1, 1, 1, GROUP * CAP, WIDE),
    )


def solution(mesh):
    return jax.shard_map(
        local,
        mesh=mesh,
        in_specs=(
            P("gx", "gy", "gz", None, None, None, None),
            P("gx", "gy", "gz", None),
            P("gx", "gy", "gz", None),
            P("gx", "gy", "gz", None),
            P("gx", "gy", "gz", None, None),
            P("gx", "gy", "gz", None, None),
        ),
        out_specs=(P("gx", "gy", "gz", None, None, None, None), P("gx", "gy", "gz", None, None)),
        check_vma=False,
    )
```

```python
import jax
import jax.numpy as jnp
from jax import lax
from jax.experimental import pallas as pl
from jax.experimental.pallas import tpu as pltpu
from jax.sharding import PartitionSpec as P

MESH = pl.DeviceIdType.MESH
EXACT = lax.Precision.HIGHEST
NY, NZ, QUAD = 4, 16, 4
HALF = NZ // 2
GROUP, CAP = 64, 2
EARLY = 8
TAG = 40
VARS, PL, NJ, NK = 5, 4, 128, 128
LINES = 64
PAD = 8
WIDE = VARS * NK
LAYER = VARS * PL
F32 = jnp.float32
ROOM = 60 * 1024 * 1024


def iota(shape, dim):
    return lax.broadcasted_iota(jnp.int32, shape, dim)


def prims(u):
    r = 1.0 / u[0]
    vel = [u[1] * r, u[2] * r, u[3] * r]
    kinetic = u[1] * vel[0] + u[2] * vel[1] + u[3] * vel[2]
    p = 0.4 * (u[4] - 0.5 * kinetic)
    return vel, p, jnp.sqrt(1.4 * p * r)


def flux(u, prim, d):
    vel, p, cs = prim
    n = vel[d]
    f = [u[1 + d]]
    for c in range(3):
        t = u[1 + c] * n
        f.append(t + p if c == d else t)
    f.append((u[4] + p) * n)
    return f, jnp.abs(n) + cs


def face(left, right):
    (ul, fl, sl), (ur, fr, sr) = left, right
    a = jnp.maximum(sl, sr)
    return [0.5 * (fl[v] + fr[v]) - 0.5 * a * (ur[v] - ul[v]) for v in range(VARS)]


def side(u, d):
    f, s = flux(u, prims(u), d)
    return u, f, s


def line_fields(dplane, dline, weights, owner):
    own_row = owner[...].astype(F32)
    earlier = iota((LINES, LINES), 0)
    later = iota((LINES, LINES), 1)
    own_col = jnp.sum(jnp.where(earlier == later, own_row, 0.0), axis=1, keepdims=True)
    rank_row = jnp.sum(
        jnp.where((own_col == own_row) & (earlier < later), 1.0, 0.0), axis=0, keepdims=True
    )
    slot_row = CAP * own_row + rank_row
    return [
        slot_row, dplane[...].astype(F32), dline[...].astype(F32), weights[0], weights[1], weights[2]
    ]


def slot_matrix(fields, lane):
    slot_row = fields[0]
    chosen = iota((GROUP * CAP, LINES), 0).astype(F32) == slot_row

    def pick(row):
        return jnp.sum(jnp.where(chosen, row, 0.0), axis=1, keepdims=True)

    q, j, a1, a2, a3 = [pick(row) for row in fields[1:]]
    used = pick(jnp.ones((1, LINES), F32))
    along_j = jnp.where(lane == j, 1.0 - a2, 0.0) + jnp.where(lane == j + 1.0, a2, 0.0)
    along_j = along_j * used
    parts = []
    for plane in range(PL):
        weight = jnp.where(q == plane, 1.0 - a1, 0.0) + jnp.where(q + 1.0 == plane, a1, 0.0)
        parts.append(weight * along_j)
    return parts, a3


def exchange_kernel(
    flow, links_in, dplane_in, dline_in, weights_in, owner_in,
    state_out, fringe_out,
    state, arrived, fringe, cells, links, dplane, dline, weights, owner,
    faces, chosen, got, ghost_lo, ghost_hi, sending, slots, rows, fracs, ends_out, ends_in, notes, tags,
    in_sem, s1_send, s1_recv, s2_send, s2_recv, m_send, m_recv, e_send, e_recv, n_send, n_recv, t_send, t_recv, f_send, f_recv, out_sem,
):
    y = lax.axis_index("gy")
    z = lax.axis_index("gz")
    me = y * NZ + z
    a, b = z % QUAD, z // QUAD

    loads = [
        pltpu.make_async_copy(flow, cells.at[:, :, pl.ds(PAD, NJ), :], in_sem.at[0]),
        pltpu.make_async_copy(links_in, links, in_sem.at[1]),
        pltpu.make_async_copy(dplane_in, dplane, in_sem.at[2]),
        pltpu.make_async_copy(dline_in, dline, in_sem.at[3]),
        pltpu.make_async_copy(weights_in, weights, in_sem.at[4]),
        pltpu.make_async_copy(owner_in, owner, in_sem.at[5]),
    ]
    for load in loads:
        load.start()

    def peer(i):
        d = HALF - (i + 4) // 8
        dz = jnp.where(i % 2 == 0, d, NZ - d)
        dy = jnp.where(d == HALF, i, jnp.where(d == 0, i - 59, (i - 4) // 2))
        return (y + dy) % NY, (z + jnp.where(d == HALF, HALF, dz)) % NZ

    barrier = pltpu.get_barrier_semaphore()

    def greet(i, carry):
        py, pz = peer(i)
        pl.semaphore_signal(barrier, inc=1, device_id={"gy": py, "gz": pz}, device_id_type=MESH)
        return carry

    lax.fori_loop(0, GROUP - 1, greet, 0)

    for load in loads:
        load.wait()

    first_last = iota((8, NK), 0)
    lane8 = iota((8, NK), 1)
    ends = jnp.where(
        ((first_last == 0) & (lane8 == 0)) | ((first_last == 1) & (lane8 == NK - 1)), 1.0, 0.0
    )
    for v in range(VARS):
        for p in range(PL):
            layer = lax.dot_general(
                ends, cells[v, p, pl.ds(PAD, NJ), :], (((1,), (1,)), ((), ())),
                precision=EXACT, preferred_element_type=F32,
            )
            faces[0, pl.ds(v * PL + p, 1), :] = layer[0:1]
            faces[0, pl.ds(LAYER + v * PL + p, 1), :] = layer[1:2]
    for r in range(2):
        tags[0, pl.ds(r, 1), :] = jnp.full((1, NJ), links[0, 2 * r], jnp.int32).astype(F32)

    lane = iota((GROUP * CAP, NK), 1)
    fields = line_fields(dplane, dline, weights, owner)
    lane_f = lane.astype(F32)
    parts, a3 = slot_matrix(fields, lane_f)
    for plane in range(PL):
        slots[:, pl.ds(plane * NJ, NJ)] = parts[plane]
    fracs[...] = jnp.broadcast_to(a3, (GROUP * CAP, NK))
    for v in range(VARS):
        lines = cells[v, :, pl.ds(PAD, NJ), :].reshape(PL * NJ, NK)
        rows[:, pl.ds(v * NK, NK)] = jnp.dot(
            slots[...], lines, precision=EXACT, preferred_element_type=F32
        )
        for p in range(PL):
            cells[v, p, pl.ds(PAD - 1, 1), :] = cells[v, p, pl.ds(PAD, 1), :]
            cells[v, p, pl.ds(PAD + NJ, 1), :] = cells[v, p, pl.ds(PAD + NJ - 1, 1), :]

    for row in range(3):
        notes[z, row] = jnp.concatenate(fields[2 * row : 2 * row + 2], axis=1)

    frac = fracs[...]
    for v in range(VARS):
        here = rows[:, pl.ds(v * NK, NK)]
        following = jnp.where(lane == NK - 1, 0.0, pltpu.roll(here, NK - 1, 1))
        value = (1.0 - frac) * here + frac * following
        sending[:, :, pl.ds(v * NK, NK)] = value.reshape(GROUP, CAP, NK)

    pl.semaphore_wait(barrier, GROUP - 1)

    def send_notes(d, carry):
        pltpu.make_async_remote_copy(
            src_ref=notes.at[z], dst_ref=notes.at[z], send_sem=n_send, recv_sem=n_recv,
            device_id={"gy": y, "gz": (z + jnp.where(d % 2 == 1, NZ - d // 2, d // 2)) % NZ},
            device_id_type=MESH,
        ).start()
        return carry

    lax.fori_loop(0, NZ - 1, lambda i, c: send_notes(NZ - i, c), 0)
    stage1 = []
    for s in range(1, QUAD):
        for buffer, send_sem, recv_sem in ((faces, s1_send, s1_recv), (tags, t_send, t_recv)):
            stage1.append(pltpu.make_async_remote_copy(
                src_ref=buffer.at[0], dst_ref=buffer.at[s],
                send_sem=send_sem.at[s], recv_sem=recv_sem.at[s],
                device_id={"gy": y, "gz": b * QUAD + (a + s) % QUAD}, device_id_type=MESH,
            ))
            stage1[-1].start()

    def send(i, carry):
        py, pz = peer(i)
        pltpu.make_async_remote_copy(
            src_ref=sending.at[py * NZ + pz], dst_ref=arrived.at[me],
            send_sem=m_send, recv_sem=m_recv,
            device_id={"gy": py, "gz": pz}, device_id_type=MESH,
        ).start()
        return carry

    lax.fori_loop(0, EARLY, send, 0)
    lane_k = iota((8, NK), 1)

    def load(at, p, shift):
        return [cells[v, p, pl.ds(at + PAD + shift, 8), :] for v in range(VARS)]

    def advance(jb, carry):
        at = pl.multiple_of(jb * 8, 8)
        centre = [load(at, p, 0) for p in range(PL)]
        prim = [prims(u) for u in centre]
        layers = [(centre[p],) + flux(centre[p], prim[p], 0) for p in range(PL)]
        edges = [layers[0][1]]
        for p in range(PL - 1):
            edges.append(face(layers[p], layers[p + 1]))
        edges.append(layers[PL - 1][1])
        for p in range(PL):
            u = centre[p]
            mid = (u,) + flux(u, prim[p], 1)
            after = face(mid, side(load(at, p, 1), 1))
            before = face(side(load(at, p, -1), 1), mid)
            for v in range(VARS):
                change = (edges[p + 1][v] - edges[p][v]) + (after[v] - before[v])
                state[v, p, pl.ds(at, 8), :] = u[v] - 0.08 * change
        return carry

    lax.fori_loop(0, NJ // 8, advance, 0)

    for copy in stage1:
        copy.wait()

    stage2 = []
    is_first = iota((2 * LAYER, NJ), 0) < LAYER
    for s in list(range(1, QUAD)) + [0]:
        goal = (((b + s) % QUAD) * QUAD + a).astype(F32)
        total = jnp.zeros((2 * LAYER, NJ), F32)
        for source in range(QUAD):
            tag = jnp.where(is_first, tags[source, pl.ds(0, 1), :], tags[source, pl.ds(1, 1), :])
            total = total + jnp.where(tag == goal, faces[source], 0.0)
        if s:
            chosen[s] = total
        else:
            got[0] = total
        if s:
            stage2.append(pltpu.make_async_remote_copy(
                src_ref=chosen.at[s], dst_ref=got.at[s],
                send_sem=s2_send.at[s], recv_sem=s2_recv.at[s],
                device_id={"gy": y, "gz": ((b + s) % QUAD) * QUAD + a}, device_id_type=MESH,
            ))
            stage2[-1].start()
    in_line = pl.ds(0, NZ - 1)
    pltpu.make_async_copy(notes.at[in_line], notes.at[in_line], n_recv).wait()
    below = jnp.full((1, 2 * LINES), links[0, 0], jnp.int32)
    theirs = []
    for row in range(3):
        wanted = jnp.zeros((1, 2 * LINES), F32)
        for source in range(NZ):
            wanted = wanted + jnp.where(below == source, notes[source, row], 0.0)
        theirs += [wanted[:, 0:LINES], wanted[:, LINES:]]
    flipped = jnp.full((GROUP * CAP, NJ), links[0, 1], jnp.int32) == 1
    parts, a3 = slot_matrix(theirs, jnp.where(flipped, NJ - 1.0 - lane_f, lane_f))
    lane_face = iota((GROUP * CAP, 2 * LAYER), 1)
    beyond = jnp.zeros((GROUP * CAP, 2 * LAYER), F32)
    for plane in range(PL):
        term = lax.dot_general(
            parts[plane], faces[0], (((1,), (1,)), ((), ())),
            precision=EXACT, preferred_element_type=F32,
        )
        beyond = beyond + jnp.where(lane_face % PL == plane, term, 0.0)
    slot = iota((GROUP * CAP, NK), 0)
    first_lane = slot // (CAP * NZ) * (CAP * VARS) + slot % CAP * VARS
    last = jnp.zeros((GROUP * CAP, NK), F32)
    for v in range(VARS):
        tail = jnp.sum(jnp.where(lane_face // PL == v, beyond, 0.0), axis=1, keepdims=True)
        last = last + jnp.where(lane == first_lane + v, a3 * tail, 0.0)
    owner_z = iota((NZ, GROUP * CAP), 1) // CAP % NZ
    by_z = jnp.dot(
        jnp.where(owner_z == iota((NZ, GROUP * CAP), 0), 1.0, 0.0), last,
        precision=EXACT, preferred_element_type=F32,
    )
    donor = jnp.full((NZ, NK), links[0, 0], jnp.int32).astype(F32)
    by_z = jnp.where(iota((NZ, NK), 1) == TAG, donor, by_z)
    for plane in range(NZ):
        ends_out[plane] = by_z[plane : plane + 1, :]

    def send_ends(d, carry):
        pz = (z + jnp.where(d % 2 == 1, NZ - d // 2, d // 2)) % NZ
        pltpu.make_async_remote_copy(
            src_ref=ends_out.at[pz], dst_ref=ends_in.at[y, z], send_sem=e_send, recv_sem=e_recv,
            device_id={"gy": y, "gz": pz}, device_id_type=MESH,
        ).start()
        return carry

    lax.fori_loop(0, NZ - 1, lambda i, c: send_ends(NZ - i, c), 0)
    ends_in[y, z] = ends_out[z]

    lax.fori_loop(EARLY, GROUP - 1, send, 0)
    arrived[me] = sending[me]

    others = pl.ds(0, GROUP - 1)
    pltpu.make_async_copy(ends_out.at[in_line], ends_out.at[in_line], e_recv).wait()
    forward = []
    for s in range(1, NY):
        forward.append(pltpu.make_async_remote_copy(
            src_ref=ends_in.at[y], dst_ref=ends_in.at[y], send_sem=f_send.at[s], recv_sem=f_recv.at[s],
            device_id={"gy": (y + s) % NY, "gz": z}, device_id_type=MESH,
        ))
        forward[-1].start()
    for copy in stage2:
        copy.wait()

    down = iota((NJ, NJ), 0)
    across = iota((NJ, NJ), 1)
    layer = (got[0] + got[1]) + (got[2] + got[3])
    for ghost, column in ((ghost_hi, 3), (ghost_lo, 1)):
        flipped = jnp.full((NJ, NJ), links[0, column], jnp.int32) == 1
        turn = jnp.where(across == jnp.where(flipped, NJ - 1 - down, down), 1.0, 0.0)
        ghost[...] = lax.dot_general(
            turn, layer, (((1,), (1,)), ((), ())), precision=EXACT, preferred_element_type=F32
        )

    def advance_k(jb, carry):
        at = pl.multiple_of(jb * 8, 8)
        lo = ghost_lo[pl.ds(at, 8), :]
        hi = ghost_hi[pl.ds(at, 8), :]
        for p in range(PL):
            u = load(at, p, 0)
            mid = side(u, 2)
            right = [
                jnp.where(lane_k == NK - 1, hi[:, v * PL + p : v * PL + p + 1], pltpu.roll(u[v], NK - 1, 1))
                for v in range(VARS)
            ]
            left = [
                jnp.where(lane_k == 0, lo[:, LAYER + v * PL + p : LAYER + v * PL + p + 1], pltpu.roll(u[v], 1, 1))
                for v in range(VARS)
            ]
            after = face(mid, side(right, 2))
            before = face(side(left, 2), mid)
            for v in range(VARS):
                old = state[v, p, pl.ds(at, 8), :]
                state[v, p, pl.ds(at, 8), :] = old - 0.08 * (after[v] - before[v])
        return carry

    lax.fori_loop(0, NJ // 8, advance_k, 0)
    put_state = pltpu.make_async_copy(state, state_out, out_sem.at[0])
    put_state.start()

    for copy in forward:
        copy.wait()
    for g in range(GROUP):
        rows[pl.ds(g, 1), pl.ds(0, NK)] = ends_in[g // NZ, g % NZ]
    came = rows[pl.ds(0, GROUP), pl.ds(0, NK)]
    source = iota((GROUP, GROUP), 0)
    place = iota((GROUP, GROUP), 1)
    donor_z = jnp.sum(jnp.where(source == place, came[:, TAG : TAG + 1], 0.0), axis=0, keepdims=True)
    donor = (place[0:1] // NZ * NZ).astype(F32) + donor_z
    move = jnp.where((iota((GROUP * CAP, GROUP), 0) // CAP).astype(F32) == donor, 1.0, 0.0)
    gained = jnp.dot(move, came, precision=EXACT, preferred_element_type=F32)
    mine = y * (CAP * VARS) + slot % CAP * VARS
    tails = [
        jnp.sum(jnp.where(lane == mine + v, gained, 0.0), axis=1, keepdims=True) for v in range(VARS)
    ]

    pltpu.make_async_copy(arrived.at[others], arrived.at[others], m_recv).wait()
    for g in range(GROUP):
        fringe[pl.ds(CAP * g, CAP), :] = arrived[g]
    for v in range(VARS):
        here = fringe[:, pl.ds(v * NK, NK)]
        fringe[:, pl.ds(v * NK, NK)] = here + jnp.where(lane == NK - 1, tails[v], 0.0)
    put_fringe = pltpu.make_async_copy(fringe, fringe_out, out_sem.at[1])
    put_fringe.start()
    pltpu.make_async_copy(sending.at[others], sending.at[others], m_send).wait()
    pltpu.make_async_copy(ends_out.at[in_line], ends_out.at[in_line], e_send).wait()
    pltpu.make_async_copy(notes.at[in_line], notes.at[in_line], n_send).wait()
    put_state.wait()
    put_fringe.wait()


def finish_kernel(state_in, fringe_in, state_out, fringe_out, state, fringe, in_sem, out_sem):
    trips = [(fringe_in, fringe, fringe_out)]
    for v in range(VARS):
        trips.append((state_in.at[v], state.at[v], state_out.at[v]))
    inward = [pltpu.make_async_copy(t[0], t[1], in_sem.at[i]) for i, t in enumerate(trips)]
    outward = [pltpu.make_async_copy(t[1], t[2], out_sem.at[i]) for i, t in enumerate(trips)]
    for copy in inward:
        copy.start()
    for first, second in zip(inward, outward):
        first.wait()
        second.start()
    for copy in outward:
        copy.wait()


def local(flow_state, face_links, donor_plane, donor_line, donor_weights, receptor_owner):
    anywhere = pl.BlockSpec(memory_space=pl.ANY)
    state, arrived = pl.pallas_call(
        exchange_kernel,
        out_shape=(
            jax.ShapeDtypeStruct((VARS, PL, NJ, NK), F32),
            jax.ShapeDtypeStruct((GROUP * CAP, WIDE), F32),
        ),
        in_specs=[anywhere] * 6,
        out_specs=(anywhere, anywhere),
        scratch_shapes=[
            pltpu.VMEM((VARS, PL, NJ, NK), F32),
            pltpu.VMEM((GROUP, CAP, WIDE), F32),
            pltpu.VMEM((GROUP * CAP, WIDE), F32),
            pltpu.VMEM((VARS, PL, NJ + 2 * PAD, NK), F32),
            pltpu.SMEM((1, 4), jnp.int32),
            pltpu.VMEM((1, LINES), jnp.int32),
            pltpu.VMEM((1, LINES), jnp.int32),
            pltpu.VMEM((3, 1, LINES), F32),
            pltpu.VMEM((1, LINES), jnp.int32),
            pltpu.VMEM((QUAD, 2 * LAYER, NJ), F32),
            pltpu.VMEM((QUAD, 2 * LAYER, NJ), F32),
            pltpu.VMEM((QUAD, 2 * LAYER, NJ), F32),
            pltpu.VMEM((NJ, 2 * LAYER), F32),
            pltpu.VMEM((NJ, 2 * LAYER), F32),
            pltpu.VMEM((GROUP, CAP, WIDE), F32),
            pltpu.VMEM((GROUP * CAP, PL * NJ), F32),
            pltpu.VMEM((GROUP * CAP, WIDE), F32),
            pltpu.VMEM((GROUP * CAP, NK), F32),
            pltpu.VMEM((NZ, 1, NK), F32),
            pltpu.VMEM((NY, NZ, 1, NK), F32),
            pltpu.VMEM((NZ, 3, 1, 2 * LINES), F32),
            pltpu.VMEM((QUAD, 2, NJ), F32),
            pltpu.SemaphoreType.DMA((6,)),
            pltpu.SemaphoreType.DMA((QUAD,)),
            pltpu.SemaphoreType.DMA((QUAD,)),
            pltpu.SemaphoreType.DMA((QUAD,)),
            pltpu.SemaphoreType.DMA((QUAD,)),
            pltpu.SemaphoreType.DMA,
            pltpu.SemaphoreType.DMA,
            pltpu.SemaphoreType.DMA,
            pltpu.SemaphoreType.DMA,
            pltpu.SemaphoreType.DMA,
            pltpu.SemaphoreType.DMA,
            pltpu.SemaphoreType.DMA((QUAD,)),
            pltpu.SemaphoreType.DMA((QUAD,)),
            pltpu.SemaphoreType.DMA((NY,)),
            pltpu.SemaphoreType.DMA((NY,)),
            pltpu.SemaphoreType.DMA((2,)),
        ],
        compiler_params=pltpu.CompilerParams(
            collective_id=0, has_side_effects=True, vmem_limit_bytes=ROOM
        ),
    )(
        flow_state.reshape(VARS, PL, NJ, NK),
        face_links.reshape(1, 4),
        donor_plane.reshape(1, LINES),
        donor_line.reshape(1, LINES),
        jnp.transpose(donor_weights, (0, 1, 4, 2, 3)).reshape(3, 1, LINES),
        receptor_owner.reshape(1, LINES),
    )
    new_state, fringe = pl.pallas_call(
        finish_kernel,
        out_shape=(
            jax.ShapeDtypeStruct((VARS, PL, NJ, NK), F32),
            jax.ShapeDtypeStruct((GROUP * CAP, WIDE), F32),
        ),
        in_specs=[anywhere, anywhere],
        out_specs=(anywhere, anywhere),
        scratch_shapes=[
            pltpu.VMEM((VARS, PL, NJ, NK), F32),
            pltpu.VMEM((GROUP * CAP, WIDE), F32),
            pltpu.SemaphoreType.DMA((1 + VARS,)),
            pltpu.SemaphoreType.DMA((1 + VARS,)),
        ],
        compiler_params=pltpu.CompilerParams(vmem_limit_bytes=ROOM),
    )(state, arrived)
    return (
        new_state.reshape(1, 1, 1, VARS, PL, NJ, NK),
        fringe.reshape(1, 1, 1, GROUP * CAP, WIDE),
    )


def solution(mesh):
    return jax.shard_map(
        local,
        mesh=mesh,
        in_specs=(
            P("gx", "gy", "gz", None, None, None, None),
            P("gx", "gy", "gz", None),
            P("gx", "gy", "gz", None),
            P("gx", "gy", "gz", None),
            P("gx", "gy", "gz", None, None),
            P("gx", "gy", "gz", None, None),
        ),
        out_specs=(P("gx", "gy", "gz", None, None, None, None), P("gx", "gy", "gz", None, None)),
        check_vma=False,
    )
```

```python
import jax
import jax.numpy as jnp
from jax import lax
from jax.experimental import pallas as pl
from jax.experimental.pallas import tpu as pltpu
from jax.sharding import PartitionSpec as P

MESH = pl.DeviceIdType.MESH
EXACT = lax.Precision.HIGHEST
NY, NZ, QUAD = 4, 16, 4
HALF = NZ // 2
GROUP, CAP = 64, 2
EARLY = 8
TAG = 40
VARS, PL, NJ, NK = 5, 4, 128, 128
LINES = 64
PAD = 8
WIDE = VARS * NK
LAYER = VARS * PL
F32 = jnp.float32
ROOM = 52 * 1024 * 1024


def iota(shape, dim):
    return lax.broadcasted_iota(jnp.int32, shape, dim)


def prims(u):
    r = 1.0 / u[0]
    vel = [u[1] * r, u[2] * r, u[3] * r]
    kinetic = u[1] * vel[0] + u[2] * vel[1] + u[3] * vel[2]
    p = 0.4 * (u[4] - 0.5 * kinetic)
    return vel, p, jnp.sqrt(1.4 * p * r)


def flux(u, prim, d):
    vel, p, cs = prim
    n = vel[d]
    f = [u[1 + d]]
    for c in range(3):
        t = u[1 + c] * n
        f.append(t + p if c == d else t)
    f.append((u[4] + p) * n)
    return f, jnp.abs(n) + cs


def face(left, right):
    (ul, fl, sl), (ur, fr, sr) = left, right
    a = jnp.maximum(sl, sr)
    return [0.5 * (fl[v] + fr[v]) - 0.5 * a * (ur[v] - ul[v]) for v in range(VARS)]


def side(u, d):
    f, s = flux(u, prims(u), d)
    return u, f, s


def line_fields(small):
    own_row = small[0]
    earlier = iota((LINES, LINES), 0)
    later = iota((LINES, LINES), 1)
    own_col = jnp.sum(jnp.where(earlier == later, own_row, 0.0), axis=1, keepdims=True)
    rank_row = jnp.sum(
        jnp.where((own_col == own_row) & (earlier < later), 1.0, 0.0), axis=0, keepdims=True
    )
    slot_row = CAP * own_row + rank_row
    return [slot_row] + [small[row] for row in range(1, 6)]


def slot_matrix(fields, lane):
    slot_row = fields[0]
    chosen = iota((GROUP * CAP, LINES), 0).astype(F32) == slot_row

    def pick(row):
        return jnp.sum(jnp.where(chosen, row, 0.0), axis=1, keepdims=True)

    q, j, a1, a2, a3 = [pick(row) for row in fields[1:]]
    used = pick(jnp.ones((1, LINES), F32))
    along_j = jnp.where(lane == j, 1.0 - a2, 0.0) + jnp.where(lane == j + 1.0, a2, 0.0)
    along_j = along_j * used
    parts = []
    for plane in range(PL):
        weight = jnp.where(q == plane, 1.0 - a1, 0.0) + jnp.where(q + 1.0 == plane, a1, 0.0)
        parts.append(weight * along_j)
    return parts, a3


def exchange_kernel(
    flow, small_in,
    state, fringe,
    arrived, cells, small,
    faces, chosen, got, ghost_lo, ghost_hi, sending, slots, rows, fracs, ends_out, ends_in, notes, tags,
    in_sem, s1_send, s1_recv, s2_send, s2_recv, m_send, m_recv, e_send, e_recv, n_send, n_recv, t_send, t_recv, f_send, f_recv,
):
    y = lax.axis_index("gy")
    z = lax.axis_index("gz")
    me = y * NZ + z
    a, b = z % QUAD, z // QUAD

    loads = [
        pltpu.make_async_copy(flow, cells.at[:, :, pl.ds(PAD, NJ), :], in_sem.at[0]),
        pltpu.make_async_copy(small_in, small, in_sem.at[1]),
    ]
    for load in loads:
        load.start()

    def peer(i):
        d = HALF - (i + 4) // 8
        dz = jnp.where(i % 2 == 0, d, NZ - d)
        dy = jnp.where(d == HALF, i, jnp.where(d == 0, i - 59, (i - 4) // 2))
        return (y + dy) % NY, (z + jnp.where(d == HALF, HALF, dz)) % NZ

    def link(shape, column):
        return jnp.broadcast_to(small[6, :, column : column + 1], shape)

    barrier = pltpu.get_barrier_semaphore()

    def greet(i, carry):
        py, pz = peer(i)
        pl.semaphore_signal(barrier, inc=1, device_id={"gy": py, "gz": pz}, device_id_type=MESH)
        return carry

    lax.fori_loop(0, GROUP - 1, greet, 0)

    for load in loads:
        load.wait()

    first_last = iota((8, NK), 0)
    lane8 = iota((8, NK), 1)
    ends = jnp.where(
        ((first_last == 0) & (lane8 == 0)) | ((first_last == 1) & (lane8 == NK - 1)), 1.0, 0.0
    )
    for v in range(VARS):
        for p in range(PL):
            layer = lax.dot_general(
                ends, cells[v, p, pl.ds(PAD, NJ), :], (((1,), (1,)), ((), ())),
                precision=EXACT, preferred_element_type=F32,
            )
            faces[0, pl.ds(v * PL + p, 1), :] = layer[0:1]
            faces[0, pl.ds(LAYER + v * PL + p, 1), :] = layer[1:2]
    for r in range(2):
        tags[0, pl.ds(r, 1), :] = link((1, NJ), 2 * r)

    lane = iota((GROUP * CAP, NK), 1)
    fields = line_fields(small)
    lane_f = lane.astype(F32)
    parts, a3 = slot_matrix(fields, lane_f)
    for plane in range(PL):
        slots[:, pl.ds(plane * NJ, NJ)] = parts[plane]
    fracs[...] = jnp.broadcast_to(a3, (GROUP * CAP, NK))
    for v in range(VARS):
        lines = cells[v, :, pl.ds(PAD, NJ), :].reshape(PL * NJ, NK)
        rows[:, pl.ds(v * NK, NK)] = jnp.dot(
            slots[...], lines, precision=EXACT, preferred_element_type=F32
        )
        for p in range(PL):
            cells[v, p, pl.ds(PAD - 1, 1), :] = cells[v, p, pl.ds(PAD, 1), :]
            cells[v, p, pl.ds(PAD + NJ, 1), :] = cells[v, p, pl.ds(PAD + NJ - 1, 1), :]

    for row in range(3):
        notes[z, row] = jnp.concatenate(fields[2 * row : 2 * row + 2], axis=1)

    frac = fracs[...]
    for v in range(VARS):
        here = rows[:, pl.ds(v * NK, NK)]
        following = jnp.where(lane == NK - 1, 0.0, pltpu.roll(here, NK - 1, 1))
        value = (1.0 - frac) * here + frac * following
        sending[:, :, pl.ds(v * NK, NK)] = value.reshape(GROUP, CAP, NK)

    pl.semaphore_wait(barrier, GROUP - 1)

    def send_notes(d, carry):
        pltpu.make_async_remote_copy(
            src_ref=notes.at[z], dst_ref=notes.at[z], send_sem=n_send, recv_sem=n_recv,
            device_id={"gy": y, "gz": (z + jnp.where(d % 2 == 1, NZ - d // 2, d // 2)) % NZ},
            device_id_type=MESH,
        ).start()
        return carry

    lax.fori_loop(0, NZ - 1, lambda i, c: send_notes(NZ - i, c), 0)
    stage1 = []
    for s in range(1, QUAD):
        for buffer, send_sem, recv_sem in ((faces, s1_send, s1_recv), (tags, t_send, t_recv)):
            stage1.append(pltpu.make_async_remote_copy(
                src_ref=buffer.at[0], dst_ref=buffer.at[s],
                send_sem=send_sem.at[s], recv_sem=recv_sem.at[s],
                device_id={"gy": y, "gz": b * QUAD + (a + s) % QUAD}, device_id_type=MESH,
            ))
            stage1[-1].start()

    def send(i, carry):
        py, pz = peer(i)
        pltpu.make_async_remote_copy(
            src_ref=sending.at[py * NZ + pz], dst_ref=arrived.at[me],
            send_sem=m_send, recv_sem=m_recv,
            device_id={"gy": py, "gz": pz}, device_id_type=MESH,
        ).start()
        return carry

    lax.fori_loop(0, EARLY, send, 0)
    lane_k = iota((8, NK), 1)

    def load(at, p, shift):
        return [cells[v, p, pl.ds(at + PAD + shift, 8), :] for v in range(VARS)]

    def advance(jb, carry):
        at = pl.multiple_of(jb * 8, 8)
        centre = [load(at, p, 0) for p in range(PL)]
        prim = [prims(u) for u in centre]
        layers = [(centre[p],) + flux(centre[p], prim[p], 0) for p in range(PL)]
        edges = [layers[0][1]]
        for p in range(PL - 1):
            edges.append(face(layers[p], layers[p + 1]))
        edges.append(layers[PL - 1][1])
        for p in range(PL):
            u = centre[p]
            mid = (u,) + flux(u, prim[p], 1)
            after = face(mid, side(load(at, p, 1), 1))
            before = face(side(load(at, p, -1), 1), mid)
            for v in range(VARS):
                change = (edges[p + 1][v] - edges[p][v]) + (after[v] - before[v])
                state[v, p, pl.ds(at, 8), :] = u[v] - 0.08 * change
        return carry

    lax.fori_loop(0, NJ // 8, advance, 0)

    for copy in stage1:
        copy.wait()

    stage2 = []
    is_first = iota((2 * LAYER, NJ), 0) < LAYER
    for s in list(range(1, QUAD)) + [0]:
        goal = (((b + s) % QUAD) * QUAD + a).astype(F32)
        total = jnp.zeros((2 * LAYER, NJ), F32)
        for source in range(QUAD):
            tag = jnp.where(is_first, tags[source, pl.ds(0, 1), :], tags[source, pl.ds(1, 1), :])
            total = total + jnp.where(tag == goal, faces[source], 0.0)
        if s:
            chosen[s] = total
        else:
            got[0] = total
        if s:
            stage2.append(pltpu.make_async_remote_copy(
                src_ref=chosen.at[s], dst_ref=got.at[s],
                send_sem=s2_send.at[s], recv_sem=s2_recv.at[s],
                device_id={"gy": y, "gz": ((b + s) % QUAD) * QUAD + a}, device_id_type=MESH,
            ))
            stage2[-1].start()
    in_line = pl.ds(0, NZ - 1)
    pltpu.make_async_copy(notes.at[in_line], notes.at[in_line], n_recv).wait()
    below = link((1, 2 * LINES), 0)
    theirs = []
    for row in range(3):
        wanted = jnp.zeros((1, 2 * LINES), F32)
        for source in range(NZ):
            wanted = wanted + jnp.where(below == source, notes[source, row], 0.0)
        theirs += [wanted[:, 0:LINES], wanted[:, LINES:]]
    flipped = link((GROUP * CAP, NJ), 1) == 1.0
    parts, a3 = slot_matrix(theirs, jnp.where(flipped, NJ - 1.0 - lane_f, lane_f))
    lane_face = iota((GROUP * CAP, 2 * LAYER), 1)
    beyond = jnp.zeros((GROUP * CAP, 2 * LAYER), F32)
    for plane in range(PL):
        term = lax.dot_general(
            parts[plane], faces[0], (((1,), (1,)), ((), ())),
            precision=EXACT, preferred_element_type=F32,
        )
        beyond = beyond + jnp.where(lane_face % PL == plane, term, 0.0)
    slot = iota((GROUP * CAP, NK), 0)
    first_lane = slot // (CAP * NZ) * (CAP * VARS) + slot % CAP * VARS
    last = jnp.zeros((GROUP * CAP, NK), F32)
    for v in range(VARS):
        tail = jnp.sum(jnp.where(lane_face // PL == v, beyond, 0.0), axis=1, keepdims=True)
        last = last + jnp.where(lane == first_lane + v, a3 * tail, 0.0)
    owner_z = iota((NZ, GROUP * CAP), 1) // CAP % NZ
    by_z = jnp.dot(
        jnp.where(owner_z == iota((NZ, GROUP * CAP), 0), 1.0, 0.0), last,
        precision=EXACT, preferred_element_type=F32,
    )
    donor = link((NZ, NK), 0)
    by_z = jnp.where(iota((NZ, NK), 1) == TAG, donor, by_z)
    for plane in range(NZ):
        ends_out[plane] = by_z[plane : plane + 1, :]

    def send_ends(d, carry):
        pz = (z + jnp.where(d % 2 == 1, NZ - d // 2, d // 2)) % NZ
        pltpu.make_async_remote_copy(
            src_ref=ends_out.at[pz], dst_ref=ends_in.at[y, z], send_sem=e_send, recv_sem=e_recv,
            device_id={"gy": y, "gz": pz}, device_id_type=MESH,
        ).start()
        return carry

    lax.fori_loop(0, NZ - 1, lambda i, c: send_ends(NZ - i, c), 0)
    ends_in[y, z] = ends_out[z]

    lax.fori_loop(EARLY, GROUP - 1, send, 0)
    arrived[me] = sending[me]

    others = pl.ds(0, GROUP - 1)
    pltpu.make_async_copy(ends_out.at[in_line], ends_out.at[in_line], e_recv).wait()
    forward = []
    for s in range(1, NY):
        forward.append(pltpu.make_async_remote_copy(
            src_ref=ends_in.at[y], dst_ref=ends_in.at[y], send_sem=f_send.at[s], recv_sem=f_recv.at[s],
            device_id={"gy": (y + s) % NY, "gz": z}, device_id_type=MESH,
        ))
        forward[-1].start()
    for copy in stage2:
        copy.wait()

    down = iota((NJ, NJ), 0)
    across = iota((NJ, NJ), 1)
    layer = (got[0] + got[1]) + (got[2] + got[3])
    for ghost, column in ((ghost_hi, 3), (ghost_lo, 1)):
        flipped = link((NJ, NJ), column) == 1.0
        turn = jnp.where(across == jnp.where(flipped, NJ - 1 - down, down), 1.0, 0.0)
        ghost[...] = lax.dot_general(
            turn, layer, (((1,), (1,)), ((), ())), precision=EXACT, preferred_element_type=F32
        )

    def advance_k(jb, carry):
        at = pl.multiple_of(jb * 8, 8)
        lo = ghost_lo[pl.ds(at, 8), :]
        hi = ghost_hi[pl.ds(at, 8), :]
        for p in range(PL):
            u = load(at, p, 0)
            mid = side(u, 2)
            right = [
                jnp.where(lane_k == NK - 1, hi[:, v * PL + p : v * PL + p + 1], pltpu.roll(u[v], NK - 1, 1))
                for v in range(VARS)
            ]
            left = [
                jnp.where(lane_k == 0, lo[:, LAYER + v * PL + p : LAYER + v * PL + p + 1], pltpu.roll(u[v], 1, 1))
                for v in range(VARS)
            ]
            after = face(mid, side(right, 2))
            before = face(side(left, 2), mid)
            for v in range(VARS):
                old = state[v, p, pl.ds(at, 8), :]
                state[v, p, pl.ds(at, 8), :] = old - 0.08 * (after[v] - before[v])
        return carry

    lax.fori_loop(0, NJ // 8, advance_k, 0)

    for copy in forward:
        copy.wait()
    for g in range(GROUP):
        rows[pl.ds(g, 1), pl.ds(0, NK)] = ends_in[g // NZ, g % NZ]
    came = rows[pl.ds(0, GROUP), pl.ds(0, NK)]
    source = iota((GROUP, GROUP), 0)
    place = iota((GROUP, GROUP), 1)
    donor_z = jnp.sum(jnp.where(source == place, came[:, TAG : TAG + 1], 0.0), axis=0, keepdims=True)
    donor = (place[0:1] // NZ * NZ).astype(F32) + donor_z
    move = jnp.where((iota((GROUP * CAP, GROUP), 0) // CAP).astype(F32) == donor, 1.0, 0.0)
    gained = jnp.dot(move, came, precision=EXACT, preferred_element_type=F32)
    mine = y * (CAP * VARS) + slot % CAP * VARS
    tails = [
        jnp.sum(jnp.where(lane == mine + v, gained, 0.0), axis=1, keepdims=True) for v in range(VARS)
    ]

    pltpu.make_async_copy(arrived.at[others], arrived.at[others], m_recv).wait()
    for g in range(GROUP):
        fringe[pl.ds(CAP * g, CAP), :] = arrived[g]
    for v in range(VARS):
        here = fringe[:, pl.ds(v * NK, NK)]
        fringe[:, pl.ds(v * NK, NK)] = here + jnp.where(lane == NK - 1, tails[v], 0.0)
    pltpu.make_async_copy(sending.at[others], sending.at[others], m_send).wait()
    pltpu.make_async_copy(ends_out.at[in_line], ends_out.at[in_line], e_send).wait()
    pltpu.make_async_copy(notes.at[in_line], notes.at[in_line], n_send).wait()


def finish_kernel(state_in, fringe_in, state_out, fringe_out, sem):
    copies = [pltpu.make_async_copy(fringe_in, fringe_out, sem.at[0])]
    for v in range(VARS):
        copies.append(pltpu.make_async_copy(state_in.at[v], state_out.at[v], sem.at[1 + v]))
    for copy in copies:
        copy.start()
    for copy in copies:
        copy.wait()


def local(flow_state, face_links, donor_plane, donor_line, donor_weights, receptor_owner):
    anywhere = pl.BlockSpec(memory_space=pl.ANY)
    vmem = pl.BlockSpec(memory_space=pltpu.VMEM)

    def at(row, values):
        after = 8 - row - values.shape[0]
        beside = LINES - values.shape[2]
        return jnp.pad(values, ((row, after), (0, 0), (0, beside)))

    whole = at(0, receptor_owner.reshape(1, 1, LINES)) + at(1, donor_plane.reshape(1, 1, LINES))
    whole = whole + at(2, donor_line.reshape(1, 1, LINES)) + at(6, face_links.reshape(1, 1, 4))
    fractions = jnp.transpose(donor_weights, (0, 1, 4, 2, 3)).reshape(3, 1, LINES)
    small = whole.astype(F32) + at(3, fractions)
    state, arrived = pl.pallas_call(
        exchange_kernel,
        out_shape=(
            jax.ShapeDtypeStruct((VARS, PL, NJ, NK), F32),
            jax.ShapeDtypeStruct((GROUP * CAP, WIDE), F32),
        ),
        in_specs=[anywhere] * 2,
        out_specs=(vmem, vmem),
        scratch_shapes=[
            pltpu.VMEM((GROUP, CAP, WIDE), F32),
            pltpu.VMEM((VARS, PL, NJ + 2 * PAD, NK), F32),
            pltpu.VMEM((8, 1, LINES), F32),
            pltpu.VMEM((QUAD, 2 * LAYER, NJ), F32),
            pltpu.VMEM((QUAD, 2 * LAYER, NJ), F32),
            pltpu.VMEM((QUAD, 2 * LAYER, NJ), F32),
            pltpu.VMEM((NJ, 2 * LAYER), F32),
            pltpu.VMEM((NJ, 2 * LAYER), F32),
            pltpu.VMEM((GROUP, CAP, WIDE), F32),
            pltpu.VMEM((GROUP * CAP, PL * NJ), F32),
            pltpu.VMEM((GROUP * CAP, WIDE), F32),
            pltpu.VMEM((GROUP * CAP, NK), F32),
            pltpu.VMEM((NZ, 1, NK), F32),
            pltpu.VMEM((NY, NZ, 1, NK), F32),
            pltpu.VMEM((NZ, 3, 1, 2 * LINES), F32),
            pltpu.VMEM((QUAD, 2, NJ), F32),
            pltpu.SemaphoreType.DMA((2,)),
            pltpu.SemaphoreType.DMA((QUAD,)),
            pltpu.SemaphoreType.DMA((QUAD,)),
            pltpu.SemaphoreType.DMA((QUAD,)),
            pltpu.SemaphoreType.DMA((QUAD,)),
            pltpu.SemaphoreType.DMA,
            pltpu.SemaphoreType.DMA,
            pltpu.SemaphoreType.DMA,
            pltpu.SemaphoreType.DMA,
            pltpu.SemaphoreType.DMA,
            pltpu.SemaphoreType.DMA,
            pltpu.SemaphoreType.DMA((QUAD,)),
            pltpu.SemaphoreType.DMA((QUAD,)),
            pltpu.SemaphoreType.DMA((NY,)),
            pltpu.SemaphoreType.DMA((NY,)),
        ],
        compiler_params=pltpu.CompilerParams(
            collective_id=0, has_side_effects=True, vmem_limit_bytes=ROOM
        ),
    )(
        flow_state.reshape(VARS, PL, NJ, NK), small
    )
    new_state, fringe = pl.pallas_call(
        finish_kernel,
        out_shape=(
            jax.ShapeDtypeStruct((VARS, PL, NJ, NK), F32),
            jax.ShapeDtypeStruct((GROUP * CAP, WIDE), F32),
        ),
        in_specs=[anywhere, anywhere],
        out_specs=(anywhere, anywhere),
        scratch_shapes=[pltpu.SemaphoreType.DMA((1 + VARS,))],
        compiler_params=pltpu.CompilerParams(vmem_limit_bytes=8 * 1024 * 1024),
    )(state, arrived)
    return (
        new_state.reshape(1, 1, 1, VARS, PL, NJ, NK),
        fringe.reshape(1, 1, 1, GROUP * CAP, WIDE),
    )


def solution(mesh):
    return jax.shard_map(
        local,
        mesh=mesh,
        in_specs=(
            P("gx", "gy", "gz", None, None, None, None),
            P("gx", "gy", "gz", None),
            P("gx", "gy", "gz", None),
            P("gx", "gy", "gz", None),
            P("gx", "gy", "gz", None, None),
            P("gx", "gy", "gz", None, None),
        ),
        out_specs=(P("gx", "gy", "gz", None, None, None, None), P("gx", "gy", "gz", None, None)),
        check_vma=False,
    )
```
